256 devices in a mesh: grp: 4 (over x), lay: 64 (over y, z, core).
Axes of the slice: x: 4, y: 4, z: 8, core: 2. Of those that a mesh axis runs over, the one named last changes fastest.
Arguments:
- weights: bfloat16 [512, 1024, 1024], P(('grp', 'lay')), may hold values from -0.1875 to 0.1875
- biases: float32 [512, 1024], P(('grp', 'lay')), may hold values from -3 to 3
- states: bfloat16 [512, 128, 1024], P(('grp', 'lay')), may hold values from -6 to 6
- guess: float32 [256, 128, 1024], P(('grp', 'lay')), may hold values from -6 to 6
- output_grad: float32 [128, 1024], replicated, may hold values from -6 to 6
- coarse_rate: float32 [256, 1024], P(('grp', 'lay')), may hold values from 0 to 1, as said below
Outputs:
- corrected: float32 [256, 128, 1024], P(('grp', 'lay'))
- weight_grads: bfloat16 [512, 1024, 1024], P(('grp', 'lay'))
- residual: float32 [256, 128, 1024], P(('grp', 'lay'))
The draws below stay inside these ranges and needn't reach their ends.
Inputs may be any that keep to these rules, and one draw needn't show every extreme that they name: `coarse_rate`: every entry is positive.
All inputs are finite; a program needn't handle non-finite values.
Results may differ from the reference program's by a relative error of at most 0.0085.
Values sent between devices are 32-bit elements; how exact they have to be, the bound alone decides.
No kernel may reach another device: no remote copies, remote signals or barrier semaphores. Data moves between devices by JAX's collectives and lax.ppermute only.
A program may use at most 320 MiB of HBM per device.

```python
import math
import jax
import jax.numpy as jnp
from jax import lax

D = 1024
BATCH = 128
LPD = 2
BLOCKS = 256
LAYERS = 512


def draw_coarse_rate(key, part):
    key = jax.random.fold_in(key, 11)
    keys = jax.random.split(key, 6)
    slow_fraction = 0.5
    slow = jax.random.uniform(keys[0], (D,), jnp.float32) < slow_fraction
    slow_rate = math.log(10.0) / BLOCKS * jax.random.uniform(keys[1], (D,), jnp.float32, 0.05, 0.25)
    fast_rate = jnp.exp(jax.random.uniform(keys[2], (D,), jnp.float32, math.log(1.0 / 50.0), math.log(1.0 / 30.0)))
    starting_level = jnp.where(slow, slow_rate, fast_rate)
    multiplier_coefficient = jnp.exp(jax.random.uniform(keys[3], (BLOCKS, D), jnp.float32, math.log(0.5), math.log(2.0)))
    spots = jax.random.randint(keys[4], (3,), 0, BLOCKS)
    match_tally = jnp.any(jnp.arange(BLOCKS)[:, None] == spots[None, :], axis=1)
    objective_measure = jax.random.uniform(keys[5], (BLOCKS, D), jnp.float32, 0.2, 0.35)
    spike_magnitude = -jnp.log(1.0 - objective_measure)
    return starting_level[None, :] * multiplier_coefficient + jnp.where(match_tally[:, None], spike_magnitude, 0.0)


def block_scale(own_key, shape, shards, least, largest):
    loudness, own = 1.0, jax.random.fold_in(own_key, 6)
    for axis_at, parts in shards:
        steps = jnp.exp(jax.random.uniform(jax.random.fold_in(own, axis_at), (parts,), jnp.float32, least / len(shards), largest / len(shards)))
        loudness = loudness * jnp.repeat(steps, shape[axis_at] // parts).reshape([-1 if axis == axis_at else 1 for axis in range(len(shape))])
    return loudness


def scatter_about(rng, shape, scale, most, shards=(), kind=jnp.bfloat16):
    entries = jax.random.normal(rng, shape, jnp.float32) * scale
    if len(shards) > 0:
        entries = block_scale(rng, shape, shards, -0.22, 0.18) * entries
    return jnp.clip(entries, min=-most, max=most).astype(kind)


def setup_inputs(seed: int = 0) -> dict:
    arg_keys = jax.random.split(jax.random.key(seed), 7)
    return {
        "weights": scatter_about(arg_keys[0], (LAYERS, D, D), D ** -0.5, 0.1875, ((0, 256),)),
        "biases": scatter_about(arg_keys[1], (LAYERS, D), 0.5, 3.0, ((0, 256),), jnp.float32),
        "states": scatter_about(arg_keys[2], (LAYERS, BATCH, D), 1.0, 6.0, ((0, 256),)),
        "guess": scatter_about(arg_keys[3], (BLOCKS, BATCH, D), 1.0, 6.0, ((0, 256),), jnp.float32),
        "output_grad": scatter_about(arg_keys[4], (BATCH, D), 1.0, 6.0, (), jnp.float32),
        "coarse_rate": draw_coarse_rate(jax.random.fold_in(arg_keys[6], 71), 0),
    }


def layer_slopes(weights_block, biases_block, states_block):
    pre = jnp.einsum("lbi,lij->lbj", states_block.astype(jnp.float32), weights_block.astype(jnp.float32)) + biases_block[:, None, :]
    act = jnp.tanh(pre)
    return 1.0 - act * act


def sweep(lam, slopes, weights_block, states_block, keep):
    grads = []
    for k in reversed(range(LPD)):
        q = (lam * slopes[k]).astype(jnp.bfloat16)
        if keep:
            g = jnp.dot(states_block[k].T, q, preferred_element_type=jnp.float32) * (0.5 / BATCH)
            grads.append(g.astype(jnp.bfloat16))
        lam = lam + 0.5 * jnp.dot(q, weights_block[k].T, preferred_element_type=jnp.float32)
    if keep:
        return jnp.stack(grads[::-1])
    return lam


def reference(weights, biases, states, guess, output_grad, coarse_rate):
    w = weights.reshape(BLOCKS, LPD, D, D)
    b = biases.reshape(BLOCKS, LPD, D)
    s = states.reshape(BLOCKS, LPD, BATCH, D)

    def propagate_state(item):
        wb, bb, sb, c = item
        return sweep(c, layer_slopes(wb, bb, sb), wb, sb, False)

    def final(item):
        wb, bb, sb, c = item
        return sweep(c, layer_slopes(wb, bb, sb), wb, sb, True)

    moved = lax.map(propagate_state, (w, b, s, guess))
    first = jnp.concatenate([moved[1:], guess[-1:]], axis=0)
    moved2 = lax.map(propagate_state, (w, b, s, first))
    residual = jnp.concatenate([moved2[1:] - first[:-1], (output_grad - first[-1])[None]], axis=0)
    multiplier_coefficient = jnp.exp(-coarse_rate)

    def chain_step(carry, item):
        fac, res = item
        value = fac[None, :] * carry + res
        return value, value

    init = jnp.zeros((BATCH, D), jnp.float32)
    discarded_output, err = lax.scan(chain_step, init, (multiplier_coefficient, residual), reverse=True)
    corrected = first + err
    grads = lax.map(final, (w, b, s, corrected))
    return corrected, grads.reshape(LAYERS, D, D), residual
```

```python
import functools

import jax
import jax.numpy as jnp
from jax import lax
from jax.experimental import pallas as pl
from jax.experimental.pallas import tpu as pltpu
from jax.sharding import Mesh, PartitionSpec as P

ALL = ("x", "y", "z", "c")
PLANE = ("y", "z")
MIB = 1024 * 1024
F32 = jnp.float32
BF16 = jnp.bfloat16
HBM = pl.BlockSpec(memory_space=pl.ANY)
VMEM = pl.BlockSpec(memory_space=pltpu.VMEM)
COLS = 512
PART = 256
ROWS = 16
PIECE = ROWS + 1
LANES = 128


def params(mib):
    return pltpu.CompilerParams(vmem_limit_bytes=mib * MIB)


def in_vmem(x):
    return pltpu.with_memory_space_constraint(x, pltpu.VMEM)


def in_hbm(x):
    return pltpu.with_memory_space_constraint(x, pltpu.HBM)


def is_top():
    top = None
    for axis in ALL:
        last = lax.axis_index(axis) == lax.axis_size(axis) - 1
        top = last if top is None else jnp.logical_and(top, last)
    return top


def times(a, b):
    return jnp.dot(a, b, preferred_element_type=F32)


def times_transposed(a, b):
    return lax.dot_general(a, b, (((1,), (1,)), ((), ())), preferred_element_type=F32)


def transposed_times(a, b):
    return lax.dot_general(a, b, (((0,), (0,)), ((), ())), preferred_element_type=F32)


def first_kernel(w, b, s, g, moved, slopes, wv, sv, gv, bv, qv, wsem, sem):
    layers, width = wv.shape[0], wv.shape[2]
    parts = width // COLS
    order = list(reversed(range(layers)))

    def chunk(l, n):
        cols = pl.ds(n * COLS, COLS)
        return pltpu.make_async_copy(w.at[l, :, cols], wv.at[l, :, cols], wsem.at[l, n])

    states = [pltpu.make_async_copy(s.at[l], sv.at[l], sem.at[l]) for l in range(layers)]
    bias = pltpu.make_async_copy(b, bv, sem.at[layers])
    guess = pltpu.make_async_copy(g.at[0], gv, sem.at[layers + 1])
    for l in order:
        states[l].start()
        for n in range(parts):
            chunk(l, n).start()
            if l == order[0] and n == 0:
                bias.start()
                guess.start()
    bias.wait()
    lam = None
    for l in order:
        states[l].wait()
        for n in range(parts):
            cols = slice(n * COLS, (n + 1) * COLS)
            chunk(l, n).wait()
            act = jnp.tanh(times(sv[l], wv[l, :, cols]) + bv[l : l + 1, cols])
            slope = 1.0 - act * act
            slopes[l, :, cols] = slope
            if lam is None:
                guess.wait()
                lam = gv
            qv[l, :, cols] = (lam[:, cols] * slope).astype(BF16)
        moved[...] = lam[...] + 0.5 * times_transposed(qv[l], wv[l])
        lam = moved


def relax(lam, slopes, wv):
    for l in reversed(range(slopes.shape[0])):
        q = (lam * slopes[l]).astype(BF16)
        lam = lam + 0.5 * times_transposed(q, wv[l])
    return lam


def second_kernel(g, og, above, rup, moved, slopes, wv, first, res, keep, send, rest, lam, extra, sem):
    top = is_top()
    half = keep.shape[1]
    batch = lam.shape[0]

    @pl.when(top)
    def _():
        one = pltpu.make_async_copy(g.at[0], lam, sem.at[0])
        two = pltpu.make_async_copy(og, extra, sem.at[1])
        one.start()
        two.start()
        one.wait()
        two.wait()
        extra[...] = extra[...] - lam[...]

    @pl.when(jnp.logical_not(top))
    def _():
        lam[...] = above[...]
        extra[...] = jnp.zeros_like(extra)

    kept = pltpu.make_async_copy(lam, first, sem.at[0])
    kept.start()
    r = relax(lam[...], slopes, wv) - moved[...]
    res[...] = r
    f = jnp.exp(-rup[...])
    v = r + f * extra[...]
    low, high = v[:, :half], v[:, half:]
    core0 = lax.axis_index("c") == 0
    keep[...] = jnp.where(core0, low, high)
    send[:batch, :] = jnp.where(core0, high, low)
    send[batch:, :] = jnp.broadcast_to(
        jnp.where(core0, f[:, half:], f[:, :half]), (send.shape[0] - batch, half)
    )
    rest[...] = high
    kept.wait()


def chip_kernel(keep, got, rate, rup, out):
    batch, half = keep.shape
    core0 = lax.axis_index("c") == 0
    own, up = jnp.exp(-rate[...]), jnp.exp(-rup[...])
    below = jnp.where(core0, up[:, :half], got[batch : batch + 1, :])
    above = jnp.where(core0, own[:, :half], up[:, half:])
    kept, other = keep[...], got[:batch, :]
    total = jnp.where(core0, kept, other) + below * jnp.where(core0, other, kept)
    factor = below * above
    blocks = half // LANES
    for j in range(out.shape[0] // PIECE):
        r, n = j // blocks, j % blocks
        cols = slice(n * LANES, (n + 1) * LANES)
        out[PIECE * j : PIECE * j + ROWS, :] = total[r * ROWS : (r + 1) * ROWS, cols]
        out[PIECE * j + ROWS : PIECE * j + PIECE, :] = factor[:, cols]


def piece(got, j):
    return got[PIECE * j : PIECE * j + ROWS, :], got[PIECE * j + ROWS : PIECE * j + PIECE, :]


def plane_kernel(got, out):
    count = got.shape[0] // PIECE
    t, f = piece(got, count - 1)
    for j in reversed(range(count - 1)):
        tj, fj = piece(got, j)
        t = tj + fj * t
        f = fj * f
    out[:ROWS, :] = t
    out[ROWS:, :] = jnp.broadcast_to(f, (8, LANES))


def scan_kernel(got, one, two, three, res, rest, out):
    del res, rest
    place, size = lax.axis_index("x"), lax.axis_size("x")
    carry = jnp.zeros((ROWS, LANES), F32)
    for k, b in ((3, three), (2, two), (1, one)):
        t, f = b[:ROWS, :], b[ROWS : ROWS + 1, :]
        carry = jnp.where(place + k < size, t + f * carry, carry)
    for j in reversed(range(out.shape[0])):
        out[j, :, :] = carry
        if j:
            t, f = piece(got, j)
            carry = t + f * carry


def fetch_kernel(first, w, s, after, first_v, wv, sv, sem):
    del after
    copies = [
        pltpu.make_async_copy(first, first_v, sem.at[0]),
        pltpu.make_async_copy(s, sv, sem.at[1]),
        pltpu.make_async_copy(w.at[pl.ds(1, wv.shape[0])], wv, sem.at[2]),
    ]
    for copy in copies:
        copy.start()
    for copy in copies:
        copy.wait()


def final_kernel(
    q_own, q_other, got, rest, rate, slopes, first, wv, sv, og, res_in,
    corrected, grads, res, lam_v, err_v, extra, gbuf, sem, gsem,
):
    top = is_top()
    core0 = lax.axis_index("c") == 0
    batch, width = lam_v.shape
    half = width // 2
    blocks = half // LANES
    layers = slopes.shape[0]

    @pl.when(top)
    def _():
        one = pltpu.make_async_copy(og, extra, sem.at[3])
        one.start()
        one.wait()

    @pl.when(top)
    def _():
        extra[...] = extra[...] - first[...]
        pltpu.make_async_copy(extra, res.at[0], sem.at[3]).start()

    @pl.when(jnp.logical_not(top))
    def _():
        extra[...] = jnp.zeros_like(extra)
        pltpu.make_async_copy(res_in, res.at[0], sem.at[3]).start()

    f = jnp.exp(-rate[...])
    for j in range(q_own.shape[0]):
        r, n = j // blocks, j % blocks
        rows = slice(r * ROWS, (r + 1) * ROWS)
        for h in range(2):
            cols = slice(h * half + n * LANES, h * half + (n + 1) * LANES)
            e = jnp.where(core0 == (h == 0), q_own[j], q_other[j])
            lower = (got, rest)[h][rows, n * LANES : (n + 1) * LANES]
            err = jnp.where(core0, f[:, cols] * e + lower, e + extra[rows, cols])
            err_v[rows, cols] = err

    lam = first[...] + err_v[...]
    lam_v[...] = lam
    keep = pltpu.make_async_copy(lam_v, corrected.at[0], sem.at[0])
    keep.start()
    parts = width // PART
    copies = []
    for l in reversed(range(layers)):
        q = (lam * slopes[l]).astype(BF16)
        for n in range(parts):
            rows = slice(n * PART, (n + 1) * PART)
            out = transposed_times(sv[l, :, rows], q) * (0.5 / batch)
            gbuf[l, rows, :] = out.astype(BF16)
            there = grads.at[l, pl.ds(n * PART, PART)]
            copy = pltpu.make_async_copy(gbuf.at[l, pl.ds(n * PART, PART)], there, gsem.at[l, n])
            copy.start()
            copies.append(copy)
        if l:
            lam = lam + 0.5 * times_transposed(q, wv[l - 1])
    keep.wait()
    pltpu.make_async_copy(extra, res.at[0], sem.at[3]).wait()
    for copy in copies:
        copy.wait()


def moved_by(array, axis, by):
    n = lax.axis_size(axis)
    return lax.ppermute(array, axis, [(i, (i + by) % n) for i in range(n)])


def moved_down(array):
    count = lax.axis_size(ALL)
    return lax.ppermute(array, ALL, [(i, i - 1) for i in range(1, count)])


def on_device(weights, biases, states, guess, output_grad, coarse_rate):
    layers, width, _ = weights.shape
    batch = states.shape[1]
    half = width // 2
    parts = width // COLS
    plane = lax.axis_size(PLANE)
    dma = pltpu.SemaphoreType.DMA
    square = jax.ShapeDtypeStruct((batch, width), F32)

    weights, biases, states = in_hbm(weights), in_hbm(biases), in_hbm(states)
    guess, output_grad = in_hbm(guess), in_hbm(output_grad)
    moved, slopes, wv = pl.pallas_call(
        first_kernel,
        out_shape=(
            square,
            pltpu.VMEM((layers, batch, width), F32),
            pltpu.VMEM(weights.shape, BF16),
        ),
        in_specs=[HBM] * 4,
        out_specs=(VMEM,) * 3,
        scratch_shapes=[
            pltpu.VMEM(states.shape, BF16),
            pltpu.VMEM((batch, width), F32),
            pltpu.VMEM(biases.shape, F32),
            pltpu.VMEM(states.shape, BF16),
            dma((layers, parts)),
            dma((layers + 2,)),
        ],
        compiler_params=params(10),
        name="first",
    )(weights, biases, states, guess)
    slopes, wv = in_vmem(slopes), in_vmem(wv)

    above = moved_down(moved)
    rup = moved_by(coarse_rate, ALL, 1)

    first, res, keep, send, rest = pl.pallas_call(
        second_kernel,
        out_shape=(
            pltpu.HBM((batch, width), F32),
            square,
            jax.ShapeDtypeStruct((batch, half), F32),
            jax.ShapeDtypeStruct((batch + 8, half), F32),
            jax.ShapeDtypeStruct((batch, half), F32),
        ),
        in_specs=[HBM] * 2 + [VMEM] * 5,
        out_specs=(HBM,) + (VMEM,) * 4,
        scratch_shapes=[pltpu.VMEM((batch, width), F32)] * 2 + [dma((2,))],
        compiler_params=params(8),
        name="second",
    )(guess, output_grad, above, rup, moved, slopes, wv)

    got = moved_by(send, "c", 1)
    pieces = pl.pallas_call(
        chip_kernel,
        out_shape=jax.ShapeDtypeStruct((plane * PIECE, LANES), F32),
        in_specs=[VMEM] * 4,
        out_specs=VMEM,
        compiler_params=params(4),
        name="chip",
    )(keep, got, coarse_rate, rup)
    pieces = pieces.reshape(plane, PIECE, 1, LANES)
    maps = lax.all_to_all(pieces, PLANE, 0, 0).reshape(plane * PIECE, LANES)
    whole = pl.pallas_call(
        plane_kernel,
        out_shape=jax.ShapeDtypeStruct((ROWS + 8, LANES), F32),
        in_specs=[VMEM],
        out_specs=VMEM,
        compiler_params=params(4),
        name="plane",
    )(maps)
    higher = [moved_by(whole, "x", -k) for k in (1, 2, 3)]
    got_rest = moved_by(rest, "c", 1)
    got_res = moved_down(res)
    entering = pl.pallas_call(
        scan_kernel,
        out_shape=jax.ShapeDtypeStruct((plane, ROWS, LANES), F32),
        in_specs=[VMEM] * 4 + [HBM] * 2,
        out_specs=VMEM,
        compiler_params=params(4),
        name="scan",
    )(maps, *higher, got_res, got_rest)
    q_own = lax.all_to_all(entering, PLANE, 0, 0)
    q_other = moved_by(q_own, "c", 1)
    first, wv, sv = pl.pallas_call(
        fetch_kernel,
        out_shape=(
            pltpu.VMEM((batch, width), F32),
            pltpu.VMEM((layers - 1, width, width), BF16),
            pltpu.VMEM(states.shape, BF16),
        ),
        in_specs=[HBM] * 4,
        out_specs=(VMEM,) * 3,
        scratch_shapes=[dma((3,))],
        compiler_params=params(4),
        cost_estimate=pl.CostEstimate(flops=0, bytes_accessed=6 * MIB, transcendentals=0),
        name="fetch",
    )(in_hbm(first), weights, states, q_own)

    return pl.pallas_call(
        final_kernel,
        out_shape=(
            jax.ShapeDtypeStruct((1, batch, width), F32),
            jax.ShapeDtypeStruct(weights.shape, BF16),
            jax.ShapeDtypeStruct((1, batch, width), F32),
        ),
        in_specs=[VMEM] * 9 + [HBM] * 2,
        out_specs=(HBM,) * 3,
        scratch_shapes=[
            pltpu.VMEM((batch, width), F32),
            pltpu.VMEM((batch, width), F32),
            pltpu.VMEM((batch, width), F32),
            pltpu.VMEM(weights.shape, BF16),
            dma((4,)),
            dma((layers, width // PART)),
        ],
        compiler_params=params(16),
        name="final",
    )(
        q_own, q_other, got, got_rest, coarse_rate, slopes,
        in_vmem(first), in_vmem(wv), in_vmem(sv), output_grad, got_res,
    )


def solution(mesh):
    devices = mesh.devices
    grid = Mesh(devices.reshape(devices.shape[0], 4, -1, 2), ALL)
    blocks = P(ALL, None, None)
    return jax.shard_map(
        on_device,
        mesh=grid,
        in_specs=(blocks, P(ALL, None), blocks, blocks, P(), P(ALL, None)),
        out_specs=(blocks, blocks, blocks),
        check_vma=False,
    )
```

```python
import functools

import jax
import jax.numpy as jnp
from jax import lax
from jax.experimental import pallas as pl
from jax.experimental.pallas import tpu as pltpu
from jax.sharding import Mesh, PartitionSpec as P

ALL = ("x", "y", "z", "c")
PLANE = ("y", "z")
MIB = 1024 * 1024
F32 = jnp.float32
BF16 = jnp.bfloat16
HBM = pl.BlockSpec(memory_space=pl.ANY)
VMEM = pl.BlockSpec(memory_space=pltpu.VMEM)
COLS = 512
PART = 256
ROWS = 16
PIECE = ROWS + 1
LANES = 128


def params(mib):
    return pltpu.CompilerParams(vmem_limit_bytes=mib * MIB)


def in_vmem(x):
    return pltpu.with_memory_space_constraint(x, pltpu.VMEM)


def in_hbm(x):
    return pltpu.with_memory_space_constraint(x, pltpu.HBM)


def is_top():
    top = None
    for axis in ALL:
        last = lax.axis_index(axis) == lax.axis_size(axis) - 1
        top = last if top is None else jnp.logical_and(top, last)
    return top


def times(a, b):
    return jnp.dot(a, b, preferred_element_type=F32)


def times_transposed(a, b):
    return lax.dot_general(a, b, (((1,), (1,)), ((), ())), preferred_element_type=F32)


def transposed_times(a, b):
    return lax.dot_general(a, b, (((0,), (0,)), ((), ())), preferred_element_type=F32)


def first_kernel(w, b, s, g, moved, slopes, wv, sv, gv, bv, qv, wsem, sem):
    layers, width = wv.shape[0], wv.shape[2]
    parts = width // COLS
    order = list(reversed(range(layers)))

    def chunk(l, n):
        cols = pl.ds(n * COLS, COLS)
        return pltpu.make_async_copy(w.at[l, :, cols], wv.at[l, :, cols], wsem.at[l, n])

    states = [pltpu.make_async_copy(s.at[l], sv.at[l], sem.at[l]) for l in range(layers)]
    bias = pltpu.make_async_copy(b, bv, sem.at[layers])
    guess = pltpu.make_async_copy(g.at[0], gv, sem.at[layers + 1])
    for l in order:
        states[l].start()
        for n in range(parts):
            chunk(l, n).start()
            if l == order[0] and n == 0:
                bias.start()
                guess.start()
    bias.wait()
    lam = None
    for l in order:
        states[l].wait()
        for n in range(parts):
            cols = slice(n * COLS, (n + 1) * COLS)
            chunk(l, n).wait()
            act = jnp.tanh(times(sv[l], wv[l, :, cols]) + bv[l : l + 1, cols])
            slope = 1.0 - act * act
            slopes[l, :, cols] = slope
            if lam is None:
                guess.wait()
                lam = gv
            qv[l, :, cols] = (lam[:, cols] * slope).astype(BF16)
        moved[...] = lam[...] + 0.5 * times_transposed(qv[l], wv[l])
        lam = moved


def relax(lam, slopes, wv):
    for l in reversed(range(slopes.shape[0])):
        q = (lam * slopes[l]).astype(BF16)
        lam = lam + 0.5 * times_transposed(q, wv[l])
    return lam


def second_kernel(g, og, above, rup, moved, slopes, wv, first, res, keep, send, rest, lam, extra, sem):
    top = is_top()
    half = keep.shape[1]
    batch = lam.shape[0]

    @pl.when(top)
    def _():
        one = pltpu.make_async_copy(g.at[0], lam, sem.at[0])
        two = pltpu.make_async_copy(og, extra, sem.at[1])
        one.start()
        two.start()
        one.wait()
        two.wait()
        extra[...] = extra[...] - lam[...]

    @pl.when(jnp.logical_not(top))
    def _():
        lam[...] = above[...]
        extra[...] = jnp.zeros_like(extra)

    kept = pltpu.make_async_copy(lam, first, sem.at[0])
    kept.start()
    r = relax(lam[...], slopes, wv) - moved[...]
    res[...] = r
    f = jnp.exp(-rup[...])
    v = r + f * extra[...]
    low, high = v[:, :half], v[:, half:]
    core0 = lax.axis_index("c") == 0
    keep[...] = jnp.where(core0, low, high)
    send[:batch, :] = jnp.where(core0, high, low)
    send[batch:, :] = jnp.broadcast_to(
        jnp.where(core0, f[:, half:], f[:, :half]), (send.shape[0] - batch, half)
    )
    rest[...] = high
    kept.wait()


def chip_kernel(keep, got, rate, rup, out):
    batch, half = keep.shape
    core0 = lax.axis_index("c") == 0
    own, up = jnp.exp(-rate[...]), jnp.exp(-rup[...])
    below = jnp.where(core0, up[:, :half], got[batch : batch + 1, :])
    above = jnp.where(core0, own[:, :half], up[:, half:])
    kept, other = keep[...], got[:batch, :]
    total = jnp.where(core0, kept, other) + below * jnp.where(core0, other, kept)
    factor = below * above
    blocks = half // LANES
    for j in range(out.shape[0] // PIECE):
        r, n = j // blocks, j % blocks
        cols = slice(n * LANES, (n + 1) * LANES)
        out[PIECE * j : PIECE * j + ROWS, :] = total[r * ROWS : (r + 1) * ROWS, cols]
        out[PIECE * j + ROWS : PIECE * j + PIECE, :] = factor[:, cols]


def piece(got, j):
    return got[PIECE * j : PIECE * j + ROWS, :], got[PIECE * j + ROWS : PIECE * j + PIECE, :]


def plane_kernel(got, out, terms, factors):
    count = terms.shape[0]
    t, f = piece(got, count - 1)
    for j in reversed(range(count)):
        if j < count - 1:
            tj, fj = piece(got, j)
            t = tj + fj * t
            f = fj * f
        terms[j, :, :] = t
        factors[j, :, :] = f
    out[:ROWS, :] = t
    out[ROWS:, :] = jnp.broadcast_to(f, (8, LANES))


def scan_kernel(terms, factors, one, two, three, res, rest, first, wv, sv, out):
    del res, rest, first, wv, sv
    place, size = lax.axis_index("x"), lax.axis_size("x")
    count = out.shape[0]
    carry = jnp.zeros((ROWS, LANES), F32)
    for k, b in ((3, three), (2, two), (1, one)):
        t, f = b[:ROWS, :], b[ROWS : ROWS + 1, :]
        carry = jnp.where(place + k < size, t + f * carry, carry)
    out[count - 1, :, :] = carry
    for j in range(count - 1):
        out[j, :, :] = terms[j + 1] + factors[j + 1] * carry


def fetch_kernel(first, w, s, after, first_v, wv, sv, sem):
    del after
    copies = [
        pltpu.make_async_copy(first, first_v, sem.at[0]),
        pltpu.make_async_copy(s, sv, sem.at[1]),
        pltpu.make_async_copy(w.at[pl.ds(1, wv.shape[0])], wv, sem.at[2]),
    ]
    for copy in copies:
        copy.start()
    for copy in copies:
        copy.wait()


def final_kernel(
    q_own, q_other, got, rest, rate, slopes, first, wv, sv, og, res_in,
    corrected, grads, res, lam_v, err_v, extra, gbuf, sem, gsem,
):
    top = is_top()
    core0 = lax.axis_index("c") == 0
    batch, width = lam_v.shape
    half = width // 2
    blocks = half // LANES
    layers = slopes.shape[0]

    @pl.when(top)
    def _():
        one = pltpu.make_async_copy(og, extra, sem.at[3])
        one.start()
        one.wait()

    @pl.when(top)
    def _():
        extra[...] = extra[...] - first[...]
        pltpu.make_async_copy(extra, res.at[0], sem.at[3]).start()

    @pl.when(jnp.logical_not(top))
    def _():
        extra[...] = jnp.zeros_like(extra)
        pltpu.make_async_copy(res_in, res.at[0], sem.at[3]).start()

    f = jnp.exp(-rate[...])
    for j in range(q_own.shape[0]):
        r, n = j // blocks, j % blocks
        rows = slice(r * ROWS, (r + 1) * ROWS)
        for h in range(2):
            cols = slice(h * half + n * LANES, h * half + (n + 1) * LANES)
            e = jnp.where(core0 == (h == 0), q_own[j], q_other[j])
            lower = (got, rest)[h][rows, n * LANES : (n + 1) * LANES]
            err = jnp.where(core0, f[:, cols] * e + lower, e + extra[rows, cols])
            err_v[rows, cols] = err

    lam = first[...] + err_v[...]
    lam_v[...] = lam
    keep = pltpu.make_async_copy(lam_v, corrected.at[0], sem.at[0])
    keep.start()
    parts = width // PART
    copies = []
    for l in reversed(range(layers)):
        q = (lam * slopes[l]).astype(BF16)
        for n in range(parts):
            rows = slice(n * PART, (n + 1) * PART)
            out = transposed_times(sv[l, :, rows], q) * (0.5 / batch)
            gbuf[l, rows, :] = out.astype(BF16)
            there = grads.at[l, pl.ds(n * PART, PART)]
            copy = pltpu.make_async_copy(gbuf.at[l, pl.ds(n * PART, PART)], there, gsem.at[l, n])
            copy.start()
            copies.append(copy)
        if l:
            lam = lam + 0.5 * times_transposed(q, wv[l - 1])
    keep.wait()
    pltpu.make_async_copy(extra, res.at[0], sem.at[3]).wait()
    for copy in copies:
        copy.wait()


def moved_by(array, axis, by):
    n = lax.axis_size(axis)
    return lax.ppermute(array, axis, [(i, (i + by) % n) for i in range(n)])


def moved_down(array):
    count = lax.axis_size(ALL)
    return lax.ppermute(array, ALL, [(i, i - 1) for i in range(1, count)])


def on_device(weights, biases, states, guess, output_grad, coarse_rate):
    layers, width, _ = weights.shape
    batch = states.shape[1]
    half = width // 2
    parts = width // COLS
    plane = lax.axis_size(PLANE)
    dma = pltpu.SemaphoreType.DMA
    square = jax.ShapeDtypeStruct((batch, width), F32)

    weights, biases, states = in_hbm(weights), in_hbm(biases), in_hbm(states)
    guess, output_grad = in_hbm(guess), in_hbm(output_grad)
    moved, slopes, wv = pl.pallas_call(
        first_kernel,
        out_shape=(
            square,
            pltpu.VMEM((layers, batch, width), F32),
            pltpu.VMEM(weights.shape, BF16),
        ),
        in_specs=[HBM] * 4,
        out_specs=(VMEM,) * 3,
        scratch_shapes=[
            pltpu.VMEM(states.shape, BF16),
            pltpu.VMEM((batch, width), F32),
            pltpu.VMEM(biases.shape, F32),
            pltpu.VMEM(states.shape, BF16),
            dma((layers, parts)),
            dma((layers + 2,)),
        ],
        compiler_params=params(10),
        name="first",
    )(weights, biases, states, guess)
    slopes, wv = in_vmem(slopes), in_vmem(wv)

    above = moved_down(moved)
    rup = moved_by(coarse_rate, ALL, 1)

    first, res, keep, send, rest = pl.pallas_call(
        second_kernel,
        out_shape=(
            pltpu.HBM((batch, width), F32),
            square,
            jax.ShapeDtypeStruct((batch, half), F32),
            jax.ShapeDtypeStruct((batch + 8, half), F32),
            jax.ShapeDtypeStruct((batch, half), F32),
        ),
        in_specs=[HBM] * 2 + [VMEM] * 5,
        out_specs=(HBM,) + (VMEM,) * 4,
        scratch_shapes=[pltpu.VMEM((batch, width), F32)] * 2 + [dma((2,))],
        compiler_params=params(8),
        name="second",
    )(guess, output_grad, above, rup, moved, slopes, wv)

    got = moved_by(send, "c", 1)
    pieces = pl.pallas_call(
        chip_kernel,
        out_shape=jax.ShapeDtypeStruct((plane * PIECE, LANES), F32),
        in_specs=[VMEM] * 4,
        out_specs=VMEM,
        compiler_params=params(4),
        name="chip",
    )(keep, got, coarse_rate, rup)
    pieces = pieces.reshape(plane, PIECE, 1, LANES)
    maps = lax.all_to_all(pieces, PLANE, 0, 0).reshape(plane * PIECE, LANES)
    whole, terms, factors = pl.pallas_call(
        plane_kernel,
        out_shape=(
            jax.ShapeDtypeStruct((ROWS + 8, LANES), F32),
            jax.ShapeDtypeStruct((plane, ROWS, LANES), F32),
            jax.ShapeDtypeStruct((plane, 1, LANES), F32),
        ),
        in_specs=[VMEM],
        out_specs=(VMEM,) * 3,
        compiler_params=params(4),
        name="plane",
    )(maps)
    higher = [moved_by(whole, "x", -k) for k in (1, 2, 3)]
    got_rest = moved_by(rest, "c", 1)
    got_res = moved_down(res)
    first, wv, sv = pl.pallas_call(
        fetch_kernel,
        out_shape=(
            pltpu.VMEM((batch, width), F32),
            pltpu.VMEM((layers - 1, width, width), BF16),
            pltpu.VMEM(states.shape, BF16),
        ),
        in_specs=[HBM] * 4,
        out_specs=(VMEM,) * 3,
        scratch_shapes=[dma((3,))],
        compiler_params=params(4),
        cost_estimate=pl.CostEstimate(flops=0, bytes_accessed=6 * MIB, transcendentals=0),
        name="fetch",
    )(in_hbm(first), weights, states, whole)
    first, wv, sv = in_vmem(first), in_vmem(wv), in_vmem(sv)
    entering = pl.pallas_call(
        scan_kernel,
        out_shape=jax.ShapeDtypeStruct((plane, ROWS, LANES), F32),
        in_specs=[VMEM] * 5 + [HBM] * 2 + [VMEM] * 3,
        out_specs=VMEM,
        compiler_params=params(4),
        name="scan",
    )(terms, factors, *higher, got_res, got_rest, first, wv, sv)
    q_own = lax.all_to_all(entering, PLANE, 0, 0)
    q_other = moved_by(q_own, "c", 1)
    return pl.pallas_call(
        final_kernel,
        out_shape=(
            jax.ShapeDtypeStruct((1, batch, width), F32),
            jax.ShapeDtypeStruct(weights.shape, BF16),
            jax.ShapeDtypeStruct((1, batch, width), F32),
        ),
        in_specs=[VMEM] * 9 + [HBM] * 2,
        out_specs=(HBM,) * 3,
        scratch_shapes=[
            pltpu.VMEM((batch, width), F32),
            pltpu.VMEM((batch, width), F32),
            pltpu.VMEM((batch, width), F32),
            pltpu.VMEM(weights.shape, BF16),
            dma((4,)),
            dma((layers, width // PART)),
        ],
        compiler_params=params(16),
        name="final",
    )(
        q_own, q_other, got, got_rest, coarse_rate, slopes,
        first, wv, sv, output_grad, got_res,
    )


def solution(mesh):
    devices = mesh.devices
    grid = Mesh(devices.reshape(devices.shape[0], 4, -1, 2), ALL)
    blocks = P(ALL, None, None)
    return jax.shard_map(
        on_device,
        mesh=grid,
        in_specs=(blocks, P(ALL, None), blocks, blocks, P(), P(ALL, None)),
        out_specs=(blocks, blocks, blocks),
        check_vma=False,
    )
```

```python
import functools

import jax
import jax.numpy as jnp
from jax import lax
from jax.experimental import pallas as pl
from jax.experimental.pallas import tpu as pltpu
from jax.sharding import Mesh, PartitionSpec as P

ALL = ("x", "y", "z", "c")
PLANE = ("y", "z")
MIB = 1024 * 1024
HALF = 512
F32 = jnp.float32
BF16 = jnp.bfloat16
HBM = pl.BlockSpec(memory_space=pl.ANY)
VMEM = pl.BlockSpec(memory_space=pltpu.VMEM)
COLS = 512
PART = 256
ROWS = 16
PIECE = ROWS + 1
LANES = 128


def params(mib):
    return pltpu.CompilerParams(vmem_limit_bytes=mib * MIB)


def in_vmem(x):
    return pltpu.with_memory_space_constraint(x, pltpu.VMEM)


def in_hbm(x):
    return pltpu.with_memory_space_constraint(x, pltpu.HBM)


def is_top():
    top = None
    for axis in ALL:
        last = lax.axis_index(axis) == lax.axis_size(axis) - 1
        top = last if top is None else jnp.logical_and(top, last)
    return top


def times(a, b):
    return jnp.dot(a, b, preferred_element_type=F32)


def times_transposed(a, b):
    return lax.dot_general(a, b, (((1,), (1,)), ((), ())), preferred_element_type=F32)


def transposed_times(a, b):
    return lax.dot_general(a, b, (((0,), (0,)), ((), ())), preferred_element_type=F32)


def first_kernel(w, b, s, g, moved, slopes, wv, sv, gv, bv, qv, wsem, sem):
    layers, width = wv.shape[0], wv.shape[2]
    parts = width // COLS
    order = list(reversed(range(layers)))

    def chunk(l, n):
        cols = pl.ds(n * COLS, COLS)
        return pltpu.make_async_copy(w.at[l, :, cols], wv.at[l, :, cols], wsem.at[l, n])

    states = [pltpu.make_async_copy(s.at[l], sv.at[l], sem.at[l]) for l in range(layers)]
    bias = pltpu.make_async_copy(b, bv, sem.at[layers])
    guess = pltpu.make_async_copy(g.at[0], gv, sem.at[layers + 1])
    for l in order:
        states[l].start()
        for n in range(parts):
            chunk(l, n).start()
            if l == order[0] and n == 0:
                bias.start()
                guess.start()
    bias.wait()
    lam = None
    for l in order:
        states[l].wait()
        for n in range(parts):
            cols = slice(n * COLS, (n + 1) * COLS)
            chunk(l, n).wait()
            act = jnp.tanh(times(sv[l], wv[l, :, cols]) + bv[l : l + 1, cols])
            slope = 1.0 - act * act
            slopes[l, :, cols] = slope
            if lam is None:
                guess.wait()
                lam = gv
            qv[l, :, cols] = (lam[:, cols] * slope).astype(BF16)
        moved[...] = lam[...] + 0.5 * times_transposed(qv[l], wv[l])
        lam = moved


def relax(lam, slopes, wv):
    for l in reversed(range(slopes.shape[0])):
        q = (lam * slopes[l]).astype(BF16)
        lam = lam + 0.5 * times_transposed(q, wv[l])
    return lam


def second_kernel(g, og, above, rup, moved, slopes, wv, first, res, keep, send, rest, lam, extra, sem):
    top = is_top()
    half = keep.shape[1]
    batch = lam.shape[0]

    @pl.when(top)
    def _():
        one = pltpu.make_async_copy(g.at[0], lam, sem.at[0])
        two = pltpu.make_async_copy(og, extra, sem.at[1])
        one.start()
        two.start()
        one.wait()
        two.wait()
        extra[...] = extra[...] - lam[...]

    @pl.when(jnp.logical_not(top))
    def _():
        lam[...] = above[...]
        extra[...] = jnp.zeros_like(extra)

    kept = pltpu.make_async_copy(lam, first, sem.at[0])
    kept.start()
    r = relax(lam[...], slopes, wv) - moved[...]
    res[...] = r
    f = jnp.exp(-rup[...])
    v = r + f * extra[...]
    low, high = v[:, :half], v[:, half:]
    core0 = lax.axis_index("c") == 0
    keep[...] = jnp.where(core0, low, high)
    send[:batch, :] = jnp.where(core0, high, low)
    send[batch:, :] = jnp.broadcast_to(
        jnp.where(core0, f[:, half:], f[:, :half]), (send.shape[0] - batch, half)
    )
    rest[...] = high
    kept.wait()


def chip_kernel(keep, got, rate, rup, out):
    batch, half = keep.shape
    core0 = lax.axis_index("c") == 0
    own, up = jnp.exp(-rate[...]), jnp.exp(-rup[...])
    below = jnp.where(core0, up[:, :half], got[batch : batch + 1, :])
    above = jnp.where(core0, own[:, :half], up[:, half:])
    kept, other = keep[...], got[:batch, :]
    total = jnp.where(core0, kept, other) + below * jnp.where(core0, other, kept)
    factor = below * above
    blocks = half // LANES
    for j in range(out.shape[0] // PIECE):
        r, n = j // blocks, j % blocks
        cols = slice(n * LANES, (n + 1) * LANES)
        out[PIECE * j : PIECE * j + ROWS, :] = total[r * ROWS : (r + 1) * ROWS, cols]
        out[PIECE * j + ROWS : PIECE * j + PIECE, :] = factor[:, cols]


def piece(got, j):
    return got[PIECE * j : PIECE * j + ROWS, :], got[PIECE * j + ROWS : PIECE * j + PIECE, :]


def plane_kernel(got, out, terms, factors):
    count = terms.shape[0]
    t, f = piece(got, count - 1)
    for j in reversed(range(count)):
        if j < count - 1:
            tj, fj = piece(got, j)
            t = tj + fj * t
            f = fj * f
        terms[j, :, :] = t
        factors[j, :, :] = f
    out[:ROWS, :] = t
    out[ROWS:, :] = jnp.broadcast_to(f, (8, LANES))


def scan_kernel(terms, factors, one, two, three, res, rest, first, wv, sv, out):
    del res, rest, first, wv, sv
    place, size = lax.axis_index("x"), lax.axis_size("x")
    count = out.shape[0]
    carry = jnp.zeros((ROWS, LANES), F32)
    for k, b in ((3, three), (2, two), (1, one)):
        t, f = b[:ROWS, :], b[ROWS : ROWS + 1, :]
        carry = jnp.where(place + k < size, t + f * carry, carry)
    out[count - 1, :, :] = carry
    for j in range(count - 1):
        out[j, :, :] = terms[j + 1] + factors[j + 1] * carry


def fetch_kernel(first, w, s, after, first_v, wv, sv, sem):
    del after
    copies = [
        pltpu.make_async_copy(first, first_v, sem.at[0]),
        pltpu.make_async_copy(s, sv, sem.at[1]),
        pltpu.make_async_copy(w.at[pl.ds(1, wv.shape[0])], wv, sem.at[2]),
    ]
    for copy in copies:
        copy.start()
    for copy in copies:
        copy.wait()


def gathered(pieces):
    blocks = HALF // LANES
    rows = [
        jnp.concatenate([pieces[r * blocks + n] for n in range(blocks)], axis=1)
        for r in range(pieces.shape[0] // blocks)
    ]
    return jnp.concatenate(rows, axis=0)


def top_extra(og, first, extra, sem):
    top = is_top()

    @pl.when(top)
    def _():
        one = pltpu.make_async_copy(og, extra, sem)
        one.start()
        one.wait()
        extra[...] = extra[...] - first[...]

    @pl.when(jnp.logical_not(top))
    def _():
        extra[...] = jnp.zeros_like(extra)


def half_product(core0, out, q, wv, k):
    top, half = wv.shape[0] - 1, q.shape[1]

    @pl.when(core0 == (k == 0))
    def _():
        out[...] = times_transposed(q[...], wv[top, :, :half])

    @pl.when(core0 != (k == 0))
    def _():
        out[...] = times_transposed(q[...], wv[top, :, half:])


def own_kernel(q_own, got, rate, slopes, first, wv, sv, og, lam_h, g_h, part, q_h, extra, sem):
    core0 = lax.axis_index("c") == 0
    batch, half = lam_h.shape
    l = slopes.shape[0] - 1
    top_extra(og, first, extra, sem.at[0])
    f = jnp.exp(-rate[...])
    e = gathered(q_own)
    err = jnp.where(core0, f[:, :half] * e + got[:batch, :], e + extra[:, half:])
    lam = jnp.where(core0, first[:, :half], first[:, half:]) + err
    lam_h[...] = lam
    q = (lam * jnp.where(core0, slopes[l, :, :half], slopes[l, :, half:])).astype(BF16)
    q_h[...] = q
    half_product(core0, part, q_h, wv, 0)
    for n in range(g_h.shape[0] // PART):
        rows = slice(n * PART, (n + 1) * PART)
        g_h[rows, :] = (transposed_times(sv[l, :, rows], q) * (0.5 / batch)).astype(BF16)


def final_kernel(
    q_other, rest, rate, slopes, first, wv, sv, lam_h, g_h, part, og, res_in,
    corrected, grads, res, lam_v, q_o, more, extra, gbuf, g_o, sem, gsem,
):
    top = is_top()
    core0 = lax.axis_index("c") == 0
    batch, width = lam_v.shape
    half = width // 2
    layers = slopes.shape[0]
    l = layers - 1
    low, high = pl.ds(0, half), pl.ds(half, half)

    def columns(buf, k):
        @pl.when(core0)
        def _():
            pltpu.make_async_copy(buf, grads.at[l, :, (low, high)[k]], sem.at[k]).start()

        @pl.when(jnp.logical_not(core0))
        def _():
            pltpu.make_async_copy(buf, grads.at[l, :, (high, low)[k]], sem.at[k]).start()

    columns(g_h, 0)
    top_extra(og, first, extra, sem.at[3])

    @pl.when(top)
    def _():
        pltpu.make_async_copy(extra, res.at[0], sem.at[3]).start()

    @pl.when(jnp.logical_not(top))
    def _():
        pltpu.make_async_copy(res_in, res.at[0], sem.at[3]).start()

    f = jnp.exp(-rate[...])
    e = gathered(q_other)
    err = jnp.where(core0, f[:, half:] * e + rest[...], e + extra[:, :half])
    other = jnp.where(core0, first[:, half:], first[:, :half]) + err
    q = (other * jnp.where(core0, slopes[l, :, half:], slopes[l, :, :half])).astype(BF16)
    q_o[...] = q
    half_product(core0, more, q_o, wv, 1)
    for n in range(width // PART):
        rows = slice(n * PART, (n + 1) * PART)
        g_o[rows, :] = (transposed_times(sv[l, :, rows], q) * (0.5 / batch)).astype(BF16)
    columns(g_o, 1)
    own = lam_h[...]
    lam_v[:, :half] = jnp.where(core0, own, other)
    lam_v[:, half:] = jnp.where(core0, other, own)
    keep = pltpu.make_async_copy(lam_v, corrected.at[0], sem.at[2])
    keep.start()
    copies = []
    lam, product = lam_v[...], part[...] + more[...]
    for k in reversed(range(l)):
        lam = lam + 0.5 * product
        q = (lam * slopes[k]).astype(BF16)
        for n in range(width // PART):
            rows = slice(n * PART, (n + 1) * PART)
            out = transposed_times(sv[k, :, rows], q) * (0.5 / batch)
            gbuf[k, rows, :] = out.astype(BF16)
            there = grads.at[k, pl.ds(n * PART, PART)]
            copy = pltpu.make_async_copy(gbuf.at[k, pl.ds(n * PART, PART)], there, gsem.at[k, n])
            copy.start()
            copies.append(copy)
        if k:
            product = times_transposed(q, wv[k - 1])
    keep.wait()
    pltpu.make_async_copy(g_h, grads.at[l, :, low], sem.at[0]).wait()
    pltpu.make_async_copy(g_o, grads.at[l, :, low], sem.at[1]).wait()
    pltpu.make_async_copy(extra, res.at[0], sem.at[3]).wait()
    for copy in copies:
        copy.wait()


def moved_by(array, axis, by):
    n = lax.axis_size(axis)
    return lax.ppermute(array, axis, [(i, (i + by) % n) for i in range(n)])


def moved_down(array):
    count = lax.axis_size(ALL)
    return lax.ppermute(array, ALL, [(i, i - 1) for i in range(1, count)])


def on_device(weights, biases, states, guess, output_grad, coarse_rate):
    layers, width, _ = weights.shape
    batch = states.shape[1]
    half = width // 2
    parts = width // COLS
    plane = lax.axis_size(PLANE)
    dma = pltpu.SemaphoreType.DMA
    square = jax.ShapeDtypeStruct((batch, width), F32)

    weights, biases, states = in_hbm(weights), in_hbm(biases), in_hbm(states)
    guess, output_grad = in_hbm(guess), in_hbm(output_grad)
    moved, slopes, wv = pl.pallas_call(
        first_kernel,
        out_shape=(
            square,
            pltpu.VMEM((layers, batch, width), F32),
            pltpu.VMEM(weights.shape, BF16),
        ),
        in_specs=[HBM] * 4,
        out_specs=(VMEM,) * 3,
        scratch_shapes=[
            pltpu.VMEM(states.shape, BF16),
            pltpu.VMEM((batch, width), F32),
            pltpu.VMEM(biases.shape, F32),
            pltpu.VMEM(states.shape, BF16),
            dma((layers, parts)),
            dma((layers + 2,)),
        ],
        compiler_params=params(10),
        name="first",
    )(weights, biases, states, guess)
    slopes, wv = in_vmem(slopes), in_vmem(wv)

    above = moved_down(moved)
    rup = moved_by(coarse_rate, ALL, 1)

    first, res, keep, send, rest = pl.pallas_call(
        second_kernel,
        out_shape=(
            pltpu.HBM((batch, width), F32),
            square,
            jax.ShapeDtypeStruct((batch, half), F32),
            jax.ShapeDtypeStruct((batch + 8, half), F32),
            jax.ShapeDtypeStruct((batch, half), F32),
        ),
        in_specs=[HBM] * 2 + [VMEM] * 5,
        out_specs=(HBM,) + (VMEM,) * 4,
        scratch_shapes=[pltpu.VMEM((batch, width), F32)] * 2 + [dma((2,))],
        compiler_params=params(8),
        name="second",
    )(guess, output_grad, above, rup, moved, slopes, wv)

    got = moved_by(send, "c", 1)
    pieces = pl.pallas_call(
        chip_kernel,
        out_shape=jax.ShapeDtypeStruct((plane * PIECE, LANES), F32),
        in_specs=[VMEM] * 4,
        out_specs=VMEM,
        compiler_params=params(4),
        name="chip",
    )(keep, got, coarse_rate, rup)
    pieces = pieces.reshape(plane, PIECE, 1, LANES)
    maps = lax.all_to_all(pieces, PLANE, 0, 0).reshape(plane * PIECE, LANES)
    whole, terms, factors = pl.pallas_call(
        plane_kernel,
        out_shape=(
            jax.ShapeDtypeStruct((ROWS + 8, LANES), F32),
            jax.ShapeDtypeStruct((plane, ROWS, LANES), F32),
            jax.ShapeDtypeStruct((plane, 1, LANES), F32),
        ),
        in_specs=[VMEM],
        out_specs=(VMEM,) * 3,
        compiler_params=params(4),
        name="plane",
    )(maps)
    higher = [moved_by(whole, "x", -k) for k in (1, 2, 3)]
    got_rest = moved_by(rest, "c", 1)
    got_res = moved_down(res)
    first, wv, sv = pl.pallas_call(
        fetch_kernel,
        out_shape=(
            pltpu.VMEM((batch, width), F32),
            pltpu.VMEM((layers - 1, width, width), BF16),
            pltpu.VMEM(states.shape, BF16),
        ),
        in_specs=[HBM] * 4,
        out_specs=(VMEM,) * 3,
        scratch_shapes=[dma((3,))],
        compiler_params=params(4),
        cost_estimate=pl.CostEstimate(flops=0, bytes_accessed=6 * MIB, transcendentals=0),
        name="fetch",
    )(in_hbm(first), weights, states, whole)
    first, wv, sv = in_vmem(first), in_vmem(wv), in_vmem(sv)
    entering = pl.pallas_call(
        scan_kernel,
        out_shape=jax.ShapeDtypeStruct((plane, ROWS, LANES), F32),
        in_specs=[VMEM] * 5 + [HBM] * 2 + [VMEM] * 3,
        out_specs=VMEM,
        compiler_params=params(4),
        name="scan",
    )(terms, factors, *higher, got_res, got_rest, first, wv, sv)
    q_own = lax.all_to_all(entering, PLANE, 0, 0)
    q_other = moved_by(q_own, "c", 1)
    lam_h, g_h, part = pl.pallas_call(
        own_kernel,
        out_shape=(
            pltpu.VMEM((batch, half), F32),
            pltpu.VMEM((width, half), BF16),
            pltpu.VMEM((batch, width), F32),
        ),
        in_specs=[VMEM] * 7 + [HBM],
        out_specs=(VMEM,) * 3,
        scratch_shapes=[pltpu.VMEM((batch, half), BF16), pltpu.VMEM((batch, width), F32), dma((1,))],
        compiler_params=params(8),
        cost_estimate=pl.CostEstimate(flops=140000000, bytes_accessed=4 * MIB, transcendentals=0),
        name="own",
    )(q_own, got, coarse_rate, slopes, first, wv, sv, output_grad)
    return pl.pallas_call(
        final_kernel,
        out_shape=(
            jax.ShapeDtypeStruct((1, batch, width), F32),
            jax.ShapeDtypeStruct(weights.shape, BF16),
            jax.ShapeDtypeStruct((1, batch, width), F32),
        ),
        in_specs=[VMEM] * 10 + [HBM] * 2,
        out_specs=(HBM,) * 3,
        scratch_shapes=[
            pltpu.VMEM((batch, width), F32),
            pltpu.VMEM((batch, half), BF16),
            pltpu.VMEM((batch, width), F32),
            pltpu.VMEM((batch, width), F32),
            pltpu.VMEM((layers - 1, width, width), BF16),
            pltpu.VMEM((width, half), BF16),
            dma((4,)),
            dma((layers - 1, width // PART)),
        ],
        compiler_params=params(14),
        name="final",
    )(
        q_other, got_rest, coarse_rate, slopes, first, wv, sv,
        in_vmem(lam_h), in_vmem(g_h), in_vmem(part), output_grad, got_res,
    )


def solution(mesh):
    devices = mesh.devices
    grid = Mesh(devices.reshape(devices.shape[0], 4, -1, 2), ALL)
    blocks = P(ALL, None, None)
    return jax.shard_map(
        on_device,
        mesh=grid,
        in_specs=(blocks, P(ALL, None), blocks, blocks, P(), P(ALL, None)),
        out_specs=(blocks, blocks, blocks),
        check_vma=False,
    )
```

```python
import functools

import jax
import jax.numpy as jnp
from jax import lax
from jax.experimental import pallas as pl
from jax.experimental.pallas import tpu as pltpu
from jax.sharding import Mesh, PartitionSpec as P

ALL = ("x", "y", "z", "c")
PLANE = ("y", "z")
MIB = 1024 * 1024
HALF = 512
F32 = jnp.float32
BF16 = jnp.bfloat16
HBM = pl.BlockSpec(memory_space=pl.ANY)
VMEM = pl.BlockSpec(memory_space=pltpu.VMEM)
COLS = 512
PART = 256
ROWS = 16
PIECE = ROWS + 1
LANES = 128


def params(mib):
    return pltpu.CompilerParams(vmem_limit_bytes=mib * MIB)


def in_vmem(x):
    return pltpu.with_memory_space_constraint(x, pltpu.VMEM)


def in_hbm(x):
    return pltpu.with_memory_space_constraint(x, pltpu.HBM)


def is_top():
    top = None
    for axis in ALL:
        last = lax.axis_index(axis) == lax.axis_size(axis) - 1
        top = last if top is None else jnp.logical_and(top, last)
    return top


def times(a, b):
    return jnp.dot(a, b, preferred_element_type=F32)


def times_transposed(a, b):
    return lax.dot_general(a, b, (((1,), (1,)), ((), ())), preferred_element_type=F32)


def transposed_times(a, b):
    return lax.dot_general(a, b, (((0,), (0,)), ((), ())), preferred_element_type=F32)


def first_kernel(w, b, s, g, moved, slopes, wv, sv, gv, bv, qv, wsem, sem):
    layers, width = wv.shape[0], wv.shape[2]
    parts = width // COLS
    order = list(reversed(range(layers)))

    def chunk(l, n):
        cols = pl.ds(n * COLS, COLS)
        return pltpu.make_async_copy(w.at[l, :, cols], wv.at[l, :, cols], wsem.at[l, n])

    states = [pltpu.make_async_copy(s.at[l], sv.at[l], sem.at[l]) for l in range(layers)]
    bias = pltpu.make_async_copy(b, bv, sem.at[layers])
    guess = pltpu.make_async_copy(g.at[0], gv, sem.at[layers + 1])
    for l in order:
        states[l].start()
        for n in range(parts):
            chunk(l, n).start()
            if l == order[0] and n == 0:
                bias.start()
                guess.start()
    bias.wait()
    lam = None
    for l in order:
        states[l].wait()
        for n in range(parts):
            cols = slice(n * COLS, (n + 1) * COLS)
            chunk(l, n).wait()
            act = jnp.tanh(times(sv[l], wv[l, :, cols]) + bv[l : l + 1, cols])
            slope = 1.0 - act * act
            slopes[l, :, cols] = slope
            if lam is None:
                guess.wait()
                lam = gv
            qv[l, :, cols] = (lam[:, cols] * slope).astype(BF16)
        moved[...] = lam[...] + 0.5 * times_transposed(qv[l], wv[l])
        lam = moved


def relax(lam, slopes, wv):
    for l in reversed(range(slopes.shape[0])):
        q = (lam * slopes[l]).astype(BF16)
        lam = lam + 0.5 * times_transposed(q, wv[l])
    return lam


def second_kernel(g, og, above, rup, moved, slopes, wv, first, res, keep, send, rest, lam, extra, sem):
    top = is_top()
    half = keep.shape[1]
    batch = lam.shape[0]

    @pl.when(top)
    def _():
        one = pltpu.make_async_copy(g.at[0], lam, sem.at[0])
        two = pltpu.make_async_copy(og, extra, sem.at[1])
        one.start()
        two.start()
        one.wait()
        two.wait()
        extra[...] = extra[...] - lam[...]

    @pl.when(jnp.logical_not(top))
    def _():
        lam[...] = above[...]
        extra[...] = jnp.zeros_like(extra)

    kept = pltpu.make_async_copy(lam, first, sem.at[0])
    kept.start()
    r = relax(lam[...], slopes, wv) - moved[...]
    res[...] = r
    f = jnp.exp(-rup[...])
    v = r + f * extra[...]
    low, high = v[:, :half], v[:, half:]
    core0 = lax.axis_index("c") == 0
    keep[...] = jnp.where(core0, low, high)
    send[:batch, :] = jnp.where(core0, high, low)
    send[batch:, :] = jnp.broadcast_to(
        jnp.where(core0, f[:, half:], f[:, :half]), (send.shape[0] - batch, half)
    )
    rest[...] = high
    kept.wait()


def chip_kernel(keep, got, rate, rup, out):
    batch, half = keep.shape
    core0 = lax.axis_index("c") == 0
    own, up = jnp.exp(-rate[...]), jnp.exp(-rup[...])
    below = jnp.where(core0, up[:, :half], got[batch : batch + 1, :])
    above = jnp.where(core0, own[:, :half], up[:, half:])
    kept, other = keep[...], got[:batch, :]
    total = jnp.where(core0, kept, other) + below * jnp.where(core0, other, kept)
    factor = below * above
    blocks = half // LANES
    for j in range(out.shape[0] // PIECE):
        r, n = j // blocks, j % blocks
        cols = slice(n * LANES, (n + 1) * LANES)
        out[PIECE * j : PIECE * j + ROWS, :] = total[r * ROWS : (r + 1) * ROWS, cols]
        out[PIECE * j + ROWS : PIECE * j + PIECE, :] = factor[:, cols]


def piece(got, j):
    return got[PIECE * j : PIECE * j + ROWS, :], got[PIECE * j + ROWS : PIECE * j + PIECE, :]


def plane_kernel(got, out, terms, factors):
    count = terms.shape[0]
    t, f = piece(got, count - 1)
    for j in reversed(range(count)):
        if j < count - 1:
            tj, fj = piece(got, j)
            t = tj + fj * t
            f = fj * f
        terms[j, :, :] = t
        factors[j, :, :] = f
    out[:ROWS, :] = t
    out[ROWS:, :] = jnp.broadcast_to(f, (8, LANES))


def scan_kernel(terms, factors, one, two, three, res, rest, first, wv, sv, out):
    del res, rest, first, wv, sv
    place, size = lax.axis_index("x"), lax.axis_size("x")
    count = out.shape[0]
    carry = jnp.zeros((ROWS, LANES), F32)
    for k, b in ((3, three), (2, two), (1, one)):
        t, f = b[:ROWS, :], b[ROWS : ROWS + 1, :]
        carry = jnp.where(place + k < size, t + f * carry, carry)
    out[count - 1, :, :] = carry
    for j in range(count - 1):
        out[j, :, :] = terms[j + 1] + factors[j + 1] * carry


def fetch_kernel(first, w, s, after, first_v, wv, sv, sem):
    del after
    copies = [
        pltpu.make_async_copy(first, first_v, sem.at[0]),
        pltpu.make_async_copy(s, sv, sem.at[1]),
        pltpu.make_async_copy(w.at[pl.ds(1, wv.shape[0])], wv, sem.at[2]),
    ]
    for copy in copies:
        copy.start()
    for copy in copies:
        copy.wait()


def gathered(pieces):
    blocks = HALF // LANES
    rows = [
        jnp.concatenate([pieces[r * blocks + n] for n in range(blocks)], axis=1)
        for r in range(pieces.shape[0] // blocks)
    ]
    return jnp.concatenate(rows, axis=0)


def top_extra(og, first, extra, sem):
    top = is_top()

    @pl.when(top)
    def _():
        one = pltpu.make_async_copy(og, extra, sem)
        one.start()
        one.wait()
        extra[...] = extra[...] - first[...]

    @pl.when(jnp.logical_not(top))
    def _():
        extra[...] = jnp.zeros_like(extra)


def own_kernel(q_own, got, rate, slopes, first, sv, og, lam_h, q_h, g_h, extra, sem):
    core0 = lax.axis_index("c") == 0
    batch, half = lam_h.shape
    l = slopes.shape[0] - 1
    top_extra(og, first, extra, sem.at[0])
    f = jnp.exp(-rate[...])
    e = gathered(q_own)
    err = jnp.where(core0, f[:, :half] * e + got[:batch, :], e + extra[:, half:])
    lam = jnp.where(core0, first[:, :half], first[:, half:]) + err
    lam_h[...] = lam
    q = (lam * jnp.where(core0, slopes[l, :, :half], slopes[l, :, half:])).astype(BF16)
    q_h[...] = q
    for n in range(g_h.shape[0] // PART):
        rows = slice(n * PART, (n + 1) * PART)
        g_h[rows, :] = (transposed_times(sv[l, :, rows], q) * (0.5 / batch)).astype(BF16)


def final_kernel(
    q_other, rest, rate, slopes, first, wv, sv, lam_h, q_h, g_h, og, res_in,
    corrected, grads, res, lam_v, q_v, extra, gbuf, g_o, sem, gsem,
):
    top = is_top()
    core0 = lax.axis_index("c") == 0
    batch, width = lam_v.shape
    half = width // 2
    layers = slopes.shape[0]
    l = layers - 1
    low, high = pl.ds(0, half), pl.ds(half, half)

    def columns(buf, k):
        @pl.when(core0)
        def _():
            pltpu.make_async_copy(buf, grads.at[l, :, (low, high)[k]], sem.at[k]).start()

        @pl.when(jnp.logical_not(core0))
        def _():
            pltpu.make_async_copy(buf, grads.at[l, :, (high, low)[k]], sem.at[k]).start()

    columns(g_h, 0)
    top_extra(og, first, extra, sem.at[3])

    @pl.when(top)
    def _():
        pltpu.make_async_copy(extra, res.at[0], sem.at[3]).start()

    @pl.when(jnp.logical_not(top))
    def _():
        pltpu.make_async_copy(res_in, res.at[0], sem.at[3]).start()

    f = jnp.exp(-rate[...])
    e = gathered(q_other)
    err = jnp.where(core0, f[:, half:] * e + rest[...], e + extra[:, :half])
    other = jnp.where(core0, first[:, half:], first[:, :half]) + err
    q = (other * jnp.where(core0, slopes[l, :, half:], slopes[l, :, :half])).astype(BF16)
    for n in range(width // PART):
        rows = slice(n * PART, (n + 1) * PART)
        g_o[rows, :] = (transposed_times(sv[l, :, rows], q) * (0.5 / batch)).astype(BF16)
    columns(g_o, 1)
    own, q_own = lam_h[...], q_h[...]
    lam_v[:, :half] = jnp.where(core0, own, other)
    lam_v[:, half:] = jnp.where(core0, other, own)
    q_v[:, :half] = jnp.where(core0, q_own, q)
    q_v[:, half:] = jnp.where(core0, q, q_own)
    keep = pltpu.make_async_copy(lam_v, corrected.at[0], sem.at[2])
    keep.start()
    copies = []
    lam, q = lam_v[...], q_v[...]
    for k in reversed(range(l)):
        lam = lam + 0.5 * times_transposed(q, wv[k])
        q = (lam * slopes[k]).astype(BF16)
        for n in range(width // PART):
            rows = slice(n * PART, (n + 1) * PART)
            out = transposed_times(sv[k, :, rows], q) * (0.5 / batch)
            gbuf[k, rows, :] = out.astype(BF16)
            there = grads.at[k, pl.ds(n * PART, PART)]
            copy = pltpu.make_async_copy(gbuf.at[k, pl.ds(n * PART, PART)], there, gsem.at[k, n])
            copy.start()
            copies.append(copy)
    keep.wait()
    pltpu.make_async_copy(g_h, grads.at[l, :, low], sem.at[0]).wait()
    pltpu.make_async_copy(g_o, grads.at[l, :, low], sem.at[1]).wait()
    pltpu.make_async_copy(extra, res.at[0], sem.at[3]).wait()
    for copy in copies:
        copy.wait()


def moved_by(array, axis, by):
    n = lax.axis_size(axis)
    return lax.ppermute(array, axis, [(i, (i + by) % n) for i in range(n)])


def moved_down(array):
    count = lax.axis_size(ALL)
    return lax.ppermute(array, ALL, [(i, i - 1) for i in range(1, count)])


def on_device(weights, biases, states, guess, output_grad, coarse_rate):
    layers, width, _ = weights.shape
    batch = states.shape[1]
    half = width // 2
    parts = width // COLS
    plane = lax.axis_size(PLANE)
    dma = pltpu.SemaphoreType.DMA
    square = jax.ShapeDtypeStruct((batch, width), F32)

    weights, biases, states = in_hbm(weights), in_hbm(biases), in_hbm(states)
    guess, output_grad = in_hbm(guess), in_hbm(output_grad)
    moved, slopes, wv = pl.pallas_call(
        first_kernel,
        out_shape=(
            square,
            pltpu.VMEM((layers, batch, width), F32),
            pltpu.VMEM(weights.shape, BF16),
        ),
        in_specs=[HBM] * 4,
        out_specs=(VMEM,) * 3,
        scratch_shapes=[
            pltpu.VMEM(states.shape, BF16),
            pltpu.VMEM((batch, width), F32),
            pltpu.VMEM(biases.shape, F32),
            pltpu.VMEM(states.shape, BF16),
            dma((layers, parts)),
            dma((layers + 2,)),
        ],
        compiler_params=params(10),
        name="first",
    )(weights, biases, states, guess)
    slopes, wv = in_vmem(slopes), in_vmem(wv)

    above = moved_down(moved)
    rup = moved_by(coarse_rate, ALL, 1)

    first, res, keep, send, rest = pl.pallas_call(
        second_kernel,
        out_shape=(
            pltpu.HBM((batch, width), F32),
            square,
            jax.ShapeDtypeStruct((batch, half), F32),
            jax.ShapeDtypeStruct((batch + 8, half), F32),
            jax.ShapeDtypeStruct((batch, half), F32),
        ),
        in_specs=[HBM] * 2 + [VMEM] * 5,
        out_specs=(HBM,) + (VMEM,) * 4,
        scratch_shapes=[pltpu.VMEM((batch, width), F32)] * 2 + [dma((2,))],
        compiler_params=params(8),
        name="second",
    )(guess, output_grad, above, rup, moved, slopes, wv)

    got = moved_by(send, "c", 1)
    pieces = pl.pallas_call(
        chip_kernel,
        out_shape=jax.ShapeDtypeStruct((plane * PIECE, LANES), F32),
        in_specs=[VMEM] * 4,
        out_specs=VMEM,
        compiler_params=params(4),
        name="chip",
    )(keep, got, coarse_rate, rup)
    pieces = pieces.reshape(plane, PIECE, 1, LANES)
    maps = lax.all_to_all(pieces, PLANE, 0, 0).reshape(plane * PIECE, LANES)
    whole, terms, factors = pl.pallas_call(
        plane_kernel,
        out_shape=(
            jax.ShapeDtypeStruct((ROWS + 8, LANES), F32),
            jax.ShapeDtypeStruct((plane, ROWS, LANES), F32),
            jax.ShapeDtypeStruct((plane, 1, LANES), F32),
        ),
        in_specs=[VMEM],
        out_specs=(VMEM,) * 3,
        compiler_params=params(4),
        name="plane",
    )(maps)
    higher = [moved_by(whole, "x", -k) for k in (1, 2, 3)]
    got_rest = moved_by(rest, "c", 1)
    got_res = moved_down(res)
    first, wv, sv = pl.pallas_call(
        fetch_kernel,
        out_shape=(
            pltpu.VMEM((batch, width), F32),
            pltpu.VMEM((layers - 1, width, width), BF16),
            pltpu.VMEM(states.shape, BF16),
        ),
        in_specs=[HBM] * 4,
        out_specs=(VMEM,) * 3,
        scratch_shapes=[dma((3,))],
        compiler_params=params(4),
        cost_estimate=pl.CostEstimate(flops=0, bytes_accessed=6 * MIB, transcendentals=0),
        name="fetch",
    )(in_hbm(first), weights, states, whole)
    first, wv, sv = in_vmem(first), in_vmem(wv), in_vmem(sv)
    entering = pl.pallas_call(
        scan_kernel,
        out_shape=jax.ShapeDtypeStruct((plane, ROWS, LANES), F32),
        in_specs=[VMEM] * 5 + [HBM] * 2 + [VMEM] * 3,
        out_specs=VMEM,
        compiler_params=params(4),
        name="scan",
    )(terms, factors, *higher, got_res, got_rest, first, wv, sv)
    q_own = lax.all_to_all(entering, PLANE, 0, 0)
    q_other = moved_by(q_own, "c", 1)
    lam_h, q_h, g_h = pl.pallas_call(
        own_kernel,
        out_shape=(
            pltpu.VMEM((batch, half), F32),
            pltpu.VMEM((batch, half), BF16),
            pltpu.VMEM((width, half), BF16),
        ),
        in_specs=[VMEM] * 6 + [HBM],
        out_specs=(VMEM,) * 3,
        scratch_shapes=[pltpu.VMEM((batch, width), F32), dma((1,))],
        compiler_params=params(8),
        cost_estimate=pl.CostEstimate(flops=140000000, bytes_accessed=4 * MIB, transcendentals=0),
        name="own",
    )(q_own, got, coarse_rate, slopes, first, sv, output_grad)
    return pl.pallas_call(
        final_kernel,
        out_shape=(
            jax.ShapeDtypeStruct((1, batch, width), F32),
            jax.ShapeDtypeStruct(weights.shape, BF16),
            jax.ShapeDtypeStruct((1, batch, width), F32),
        ),
        in_specs=[VMEM] * 10 + [HBM] * 2,
        out_specs=(HBM,) * 3,
        scratch_shapes=[
            pltpu.VMEM((batch, width), F32),
            pltpu.VMEM((batch, width), BF16),
            pltpu.VMEM((batch, width), F32),
            pltpu.VMEM((layers - 1, width, width), BF16),
            pltpu.VMEM((width, half), BF16),
            dma((4,)),
            dma((layers - 1, width // PART)),
        ],
        compiler_params=params(14),
        name="final",
    )(
        q_other, got_rest, coarse_rate, slopes, first, wv, sv,
        in_vmem(lam_h), in_vmem(q_h), in_vmem(g_h), output_grad, got_res,
    )


def solution(mesh):
    devices = mesh.devices
    grid = Mesh(devices.reshape(devices.shape[0], 4, -1, 2), ALL)
    blocks = P(ALL, None, None)
    return jax.shard_map(
        on_device,
        mesh=grid,
        in_specs=(blocks, P(ALL, None), blocks, blocks, P(), P(ALL, None)),
        out_specs=(blocks, blocks, blocks),
        check_vma=False,
    )
```
